32 devices in a mesh: groups: 2 (over x), ep: 16 (over z, y, core).
Axes of the slice: x: 2, y: 2, z: 4, core: 2. Of those that a mesh axis runs over, the one named last changes fastest.
Arguments:
- tokens: bfloat16 [2048, 3584], P(('groups', 'ep')), parts along dimension 0, may hold values from -6 to 6
- w_gate_up: bfloat16 [16, 3584, 512], P('ep'), may hold values from -0.09375 to 0.09375
- w_down: bfloat16 [16, 256, 3584], P('ep'), may hold values from -0.1875 to 0.1875
- w_copy_gate_up: bfloat16 [16, 3584, 512], P('ep'), may hold values from -0.09375 to 0.09375
- w_copy_down: bfloat16 [16, 256, 3584], P('ep'), may hold values from -0.1875 to 0.1875
- routes: int32 [2048, 2], P(('groups', 'ep')), parts along dimension 0, may hold values from 0 to 7, all different within a row; in each aligned block of 64 rows (0 to 63, 64 to 127, ...) at most 20 rows name the same one
- gate_weights: float32 [2048, 2], P(('groups', 'ep')), parts along dimension 0, may hold values from 0.1 to 1
- counts: int32 [32], P(('groups', 'ep')), parts along dimension 0, may hold values from 1 to 64, 768 in all
Outputs:
- moe_output: bfloat16 [2048, 3584], P(('groups', 'ep')), parts along dimension 0
The draws below stay inside these ranges and needn't reach their ends.
There are 2 independent parts, one for each index of `groups`. The reference program is written for one: setup_inputs(seed, part) draws one part's arguments, and reference() takes and returns one part's arrays. A program takes and returns all parts, laid end to end along the dimension named above; an argument that names none is the same for every part. Nothing has to cross between parts.
Inputs may be any that keep to these rules, and one draw needn't show every extreme that they name: `routes`: each row names 2 different instances. Instances i and 4 + i live on devices 4 * i to 4 * i + 4 - 1 (team i). Among the rows of one device no instance is named by more than 20 rows.
All inputs are finite; a program needn't handle non-finite values. No bound on the sum of `counts` on one device may be relied on, other than what follows from the above.
Results may differ from the reference program's by a relative error of at most 0.0058.
Values may be sent and summed in bfloat16 or wider, within the bound.
A program may use at most 128 MiB of HBM per device.

```python
import math
import jax
import jax.numpy as jnp
import numpy as np
from jax import lax

D = 3584
H = 1024
SPLIT = 4
TOP = 2
TOK_DEV = 64
HS = 256
EXPERTS = 4
CAP = 20
TOKENS = 1024
N_EP = 16


def block_levels(stream_key, shape, split, low, top_value):
    gain, own = 1.0, jax.random.fold_in(stream_key, 6)
    for dim, parts in split:
        heights = jnp.exp(jax.random.uniform(jax.random.fold_in(own, dim), (parts,), jnp.float32, low / len(split), top_value / len(split)))
        gain = gain * jnp.repeat(heights, shape[dim] // parts).reshape([-1 if axis == dim else 1 for axis in range(len(shape))])
    return gain


def split_up(number_of, total, reach, skew):
    loads = [(1 << 20) // math.isqrt(grade ** skew) + 1 for grade in range(2, number_of + 1)]
    rest, holding = total - reach - (number_of - 1), [1] * (number_of - 1)
    while rest > 0:
        movable = [i for i in range(number_of - 1) if holding[i] < reach]
        whole, budget = sum([loads[i] for i in movable]), rest
        for i in movable:
            addition = min(reach - holding[i], max(1, budget * loads[i] // whole), rest)
            holding[i] = holding[i] + addition
            rest = rest - addition
    return np.array([reach] + holding)


def ragged(own_key, count, total, bound, slope):
    if count == 2:
        one = jax.random.randint(own_key, (), max(1, total - bound), min(bound, total - 1) + 1)
        return jnp.stack([one, total - one])
    tallies = jnp.asarray(split_up(count, total, bound, slope), jnp.int32)
    couples = (count - 1) // 2
    donor, receiver = tallies[1:1 + 2 * couples:2], tallies[2:2 + 2 * couples:2]
    room = jnp.minimum(donor - 1, bound - receiver)
    moved = jax.random.randint(jax.random.fold_in(own_key, 1), (couples,), 0, 1 << 20) % (room + 1)
    tallies = tallies.at[1:1 + 2 * couples:2].set(donor - moved).at[2:2 + 2 * couples:2].set(receiver + moved)
    return tallies[jax.random.permutation(jax.random.fold_in(own_key, 2), count)]


def deal_out(own_key, own, number, rows, amount, top, reach, slope):
    sequence = jax.random.permutation(own_key, amount)
    heavy_load, ordinary = portions_of(amount, rows * top, reach, slope, True), portions_of(amount, rows * top, reach, slope, False)
    places = jnp.arange(amount)

    def named(lengths, rotation):
        used = int((lengths > 0).sum())
        fixed = max(1, used // 4)
        moved = fixed + (places - fixed + rotation * (used - fixed)) % max(1, amount - fixed)
        return jnp.zeros((amount,), jnp.int32).at[sequence[jnp.where(places < fixed, places, moved)]].set(jnp.asarray(lengths, jnp.int32))

    lengths = jnp.where(number % 4 == 0, named(heavy_load, number // 4), named(ordinary, number - number // 4 - 1))
    mixed = jax.random.permutation(jax.random.fold_in(own, 3), amount)
    giver, taker = mixed[0:amount // 2 * 2:2], mixed[1:amount // 2 * 2:2]
    room = jnp.minimum(lengths[giver] - 1, reach - lengths[taker]) // 2
    room = jnp.where((giver == sequence[0]) | (taker == sequence[0]) | (lengths[taker] == 0), 0, jnp.maximum(room, 0))
    moved = jax.random.randint(jax.random.fold_in(own, 4), (amount // 2,), 0, 1 << 20) % (room + 1)
    lengths = lengths.at[giver].add(-moved).at[taker].add(moved)
    labels = jnp.searchsorted(jnp.cumsum(lengths), jnp.arange(rows * top), side="right").astype(jnp.int32)
    table = labels.reshape(top, rows).T
    table = table[jax.random.permutation(jax.random.fold_in(own, 1), rows)]
    rotation = jax.random.randint(jax.random.fold_in(own, 2), (rows, 1), 0, top)
    return jnp.take_along_axis(table, (jnp.arange(top)[None, :] + rotation) % top, axis=1)


def portions_of(count, total, bound, slope, full):
    weights = [(1 << 20) // math.isqrt(grade ** slope) + 1 for grade in range(1, count + 1)]
    largest = bound if full else min(bound, max(-(-total // count), total * weights[0] // sum(weights)))
    least = 1 if total - largest >= count - 1 else 0
    holding, rest = [largest] + [least] * (count - 1), total - largest - least * (count - 1)
    while rest > 0:
        free = [i for i in range(1, count) if holding[i] < largest] or [i for i in range(1, count) if holding[i] < bound]
        mass, remaining = sum([weights[i] for i in free]), rest
        for i in free:
            extra = min(bound - holding[i], max(1, remaining * weights[i] // mass), rest)
            holding[i] = holding[i] + extra
            rest = rest - extra
    return np.array(holding)


def bell_draw(key, extent, spread, reach, shards=(), held_as=jnp.bfloat16):
    values = jax.random.normal(key, extent, jnp.float32) * spread
    if len(shards) > 0:
        values = block_levels(key, extent, shards, -0.22, 0.18) * values
    return jnp.clip(values, min=-reach, max=reach).astype(held_as)


def setup_inputs(seed: int = 0, part: int = 0) -> dict:
    keys = jax.random.split(jax.random.key(seed), 9)
    own_keys = jax.random.split(jax.random.fold_in(keys[8], part), 9)
    tokens = bell_draw(own_keys[0], (TOKENS, D), 1.0, 6.0, ((0, 16),))
    w_gate_up = bell_draw(keys[1], (EXPERTS * SPLIT, D, 2 * HS), D ** -0.5, 0.09375, ((0, 16),))
    w_down = bell_draw(keys[2], (EXPERTS * SPLIT, HS, D), H ** -0.5, 0.1875, ((0, 16),))
    w_copy_gate_up = bell_draw(keys[3], (EXPERTS * SPLIT, D, 2 * HS), D ** -0.5, 0.09375, ((0, 16),))
    w_copy_down = bell_draw(keys[4], (EXPERTS * SPLIT, HS, D), H ** -0.5, 0.1875, ((0, 16),))
    routes_keys = jax.random.split(jax.random.fold_in(own_keys[5], 1), TOKENS // TOK_DEV)
    routes_turns = jax.random.permutation(jax.random.fold_in(own_keys[5], 3), TOKENS // TOK_DEV)
    routes = jax.vmap(lambda own, number: deal_out(jax.random.fold_in(own_keys[5], 2), own, number, TOK_DEV, 2 * EXPERTS, TOP, CAP, 1))(routes_keys, routes_turns).reshape((TOKENS, TOP))
    gate_weights = jnp.clip(0.1 + 0.9 * jax.random.uniform(own_keys[6], (TOKENS, TOP), jnp.float32) ** block_levels(own_keys[6], (TOKENS, TOP), ((0, 16),), -0.2, 0.2), 0.1, 1.0)
    counts = ragged(own_keys[7], N_EP, 3 * TOKENS // 4, TOK_DEV, 1).astype(jnp.int32)
    return {"tokens": tokens, "w_gate_up": w_gate_up, "w_down": w_down, "w_copy_gate_up": w_copy_gate_up, "w_copy_down": w_copy_down, "routes": routes, "gate_weights": gate_weights, "counts": counts}


def expert_rows(token_rows, gate_up_proj, down_proj):
    projected = jnp.dot(token_rows, gate_up_proj, preferred_element_type=jnp.float32)
    hidden = (jax.nn.silu(projected[:, :HS]) * projected[:, HS:]).astype(jnp.bfloat16)
    return jnp.dot(hidden, down_proj, preferred_element_type=jnp.float32).astype(jnp.bfloat16)


def reference(tokens, w_gate_up, w_down, w_copy_gate_up, w_copy_down, routes, gate_weights, counts):
    entries = TOKENS * TOP
    flat_routes = routes.reshape(-1)
    token_of = (jnp.arange(entries, dtype=jnp.int32) // TOP).astype(jnp.int32)
    positions = jnp.arange(TOKENS, dtype=jnp.int32)
    live_rows = (positions % TOK_DEV) < counts[positions // TOK_DEV]
    alive_entry = live_rows[token_of]
    weight = jnp.where(alive_entry, gate_weights.reshape(-1), 0.0)
    slot_bound = N_EP * CAP

    def one_instance(accumulated, instance):
        first_kind = instance < EXPERTS
        team = (instance % EXPERTS).astype(jnp.int32)
        chosen = (flat_routes == instance) & alive_entry
        position = jnp.cumsum(chosen.astype(jnp.int32)) - 1
        target = jnp.where(chosen, position, slot_bound).astype(jnp.int32)
        entry_index = jnp.zeros((slot_bound + 1,), jnp.int32).at[target].set(jnp.arange(entries, dtype=jnp.int32))[:slot_bound]
        in_use = jnp.arange(slot_bound, dtype=jnp.int32) < jnp.sum(chosen.astype(jnp.int32))
        token_rows = tokens[token_of[entry_index]]
        summed = jnp.zeros((slot_bound, D), jnp.float32)
        for quarter in range(SPLIT):
            weight_slot = (team * SPLIT + quarter).astype(jnp.int32)
            gate_up_proj = jnp.where(first_kind, lax.dynamic_index_in_dim(w_gate_up, weight_slot, 0, keepdims=False), lax.dynamic_index_in_dim(w_copy_gate_up, weight_slot, 0, keepdims=False))
            down_proj = jnp.where(first_kind, lax.dynamic_index_in_dim(w_down, weight_slot, 0, keepdims=False), lax.dynamic_index_in_dim(w_copy_down, weight_slot, 0, keepdims=False))
            summed = summed + expert_rows(token_rows, gate_up_proj, down_proj).astype(jnp.float32)
        row_scale = jnp.where(in_use, weight[entry_index], 0.0)
        accumulated = accumulated.at[token_of[entry_index]].add(summed * row_scale[:, None])
        return accumulated, None

    accumulated, _ = lax.scan(one_instance, jnp.zeros((TOKENS, D), jnp.float32), jnp.arange(2 * EXPERTS, dtype=jnp.int32))
    return accumulated.astype(jnp.bfloat16)
```

```python
import functools

import jax
import jax.numpy as jnp
from jax import lax
from jax.experimental import pallas as pl
from jax.experimental.pallas import tpu as pltpu
from jax.sharding import PartitionSpec as P

MESH = pl.DeviceIdType.MESH
BF = jnp.bfloat16
F32 = jnp.float32


def dot(a, b):
    return jnp.dot(a, b, preferred_element_type=F32)


def dot_nt(a, b):
    return lax.dot_general(a, b, (((1,), (1,)), ((), ())), preferred_element_type=F32)


def kernel(
    T, CAP, R, LO, HI,
    tok_ref, wg_ref, wd_ref, cg_ref, cd_ref, rt_ref, gw_ref, cnt_ref,
    out_ref,
    wg, wd, stk, gm, xs, X, pw, ps, pr, own, ys, yr, ks, zs, ret, fin,
    lsem, wsem, xsend, xrecv, tsend, trecv, dsem,
):
    TOK = tok_ref.shape[0]
    D = tok_ref.shape[1]
    H = D // 2
    HS = wd.shape[2]
    ep = lax.axis_index("ep")
    z = ep // 4
    y = (ep // 2) % 2
    c = ep % 2
    e_core = ep + 1 - 2 * c
    e_y = ep + 2 - 4 * y

    def src_plane(g):
        return lax.rem(z + g, T)

    def dst_plane(g):
        return lax.rem(z + T - g, T)

    def remote(src, dst, ssem, rsem, dev):
        return pltpu.make_async_remote_copy(
            src_ref=src, dst_ref=dst, send_sem=ssem, recv_sem=rsem,
            device_id={"ep": dev}, device_id_type=MESH,
        )

    def half(i):
        return pl.ds(pl.multiple_of(i * H, 128), H)

    wcopies = []
    for a, (gr, dr) in enumerate(((wg_ref, wd_ref), (cg_ref, cd_ref))):
        for h in range(2):
            wcopies.append(pltpu.make_async_copy(
                gr.at[0, pl.ds(h * H, H), :], wg.at[a, h], wsem.at[2 * a + h]))
            wcopies.append(pltpu.make_async_copy(
                dr.at[0, :, pl.ds(h * H, H)], wd.at[a, h], wsem.at[4 + 2 * a + h]))
    rows = pl.ds(pl.multiple_of(c * TOK, 16), TOK)
    lcopy = pltpu.make_async_copy(tok_ref.at[:, half(c)], stk.at[rows, :], lsem.at[0])
    lcopy.start()

    barrier = pltpu.get_barrier_semaphore()
    for g in range(1, T):
        pl.semaphore_signal(barrier, inc=1, device_id={"ep": lax.rem(z + g, T) * 4 + lax.rem(ep, 4)},
                            device_id_type=MESH)
    pl.semaphore_signal(barrier, inc=1, device_id={"ep": e_core}, device_id_type=MESH)
    pl.semaphore_signal(barrier, inc=1, device_id={"ep": e_y}, device_id_type=MESH)

    lane = lax.broadcasted_iota(jnp.int32, (TOK, 128), 1)
    row = lax.broadcasted_iota(jnp.int32, (TOK, 128), 0)
    live = row < cnt_ref[0]
    r0 = jnp.broadcast_to(rt_ref[:, 0:1], (TOK, 128))
    r1 = jnp.broadcast_to(rt_ref[:, 1:2], (TOK, 128))
    g0 = jnp.broadcast_to(gw_ref[:, 0:1], (TOK, 128))
    g1 = jnp.broadcast_to(gw_ref[:, 1:2], (TOK, 128))
    member = (lane == r0) | (lane == r1)
    gate = jnp.where(lane == r0 + 64, g0, jnp.where(lane == r1 + 64, g1, 0.0))
    mine = jnp.where(live, jnp.where(member, 1.0, gate), 0.0)
    mrow = pl.ds(pl.multiple_of(c * TOK, 16), TOK)
    gm[mrow, :] = mine

    pl.semaphore_wait(barrier, T + 1)

    tcopy = remote(tok_ref.at[:, half(1 - c)], stk.at[rows, :], tsend.at[0], trecv.at[0], e_core)
    mcopy = remote(gm.at[mrow, :], gm.at[mrow, :], tsend.at[1], trecv.at[1], e_core)
    mcopy.start()
    tcopy.start()
    for w in wcopies:
        w.start()

    n2 = 2 * TOK
    p = lax.broadcasted_iota(jnp.int32, (T, R, 128), 1).reshape(T * R, 128)
    team = lax.broadcasted_iota(jnp.int32, (T, R, 128), 0).reshape(T * R, 128)
    ln = lax.broadcasted_iota(jnp.int32, (T * R, 128), 1)
    one = lambda m: jnp.where(m, 1, 0)
    q = one(p >= CAP) + one(p >= 2 * CAP) + one(p >= 3 * CAP)
    copy_i = one(p >= 2 * CAP)
    core_i = q - 2 * copy_i
    rank_i = p - q * CAP
    valid = p < 4 * CAP
    inst = copy_i * T + team
    sel = jnp.where((ln == inst) & valid, 1.0, 0.0).astype(BF)
    selg = jnp.where((ln == inst + 64) & valid, 1.0, 0.0).astype(BF)
    tcore = one(ln >= TOK)
    ta = lax.broadcasted_iota(jnp.int32, (n2, n2), 0)
    tb = lax.broadcasted_iota(jnp.int32, (n2, n2), 1)
    low = jnp.where((tb < ta) & ((tb >= TOK) == (ta >= TOK)), 1.0, 0.0).astype(BF)

    mcopy.wait_recv()
    gall = gm[...]
    ghi = gall.astype(BF)
    glo = (gall - ghi.astype(F32)).astype(BF)
    rank = dot(low, ghi)
    a_m = dot_nt(sel, ghi)
    a_r = dot_nt(sel, rank.astype(BF))
    pick = (a_m > 0.5) & (a_r == rank_i.astype(F32)) & (tcore == core_i)
    pick = jnp.where(pick, 1.0, 0.0)
    pw[0] = (pick * dot_nt(selg, ghi)).astype(BF)
    pw[1] = (pick * dot_nt(selg, glo)).astype(BF)
    pw[2] = pick.astype(BF)
    lcopy.wait()
    tcopy.wait_recv()

    def zsend(g):
        return remote(xs.at[dst_plane(g)], X.at[z, y, c], xsend.at[0, g], xrecv.at[0, g],
                      dst_plane(g) * 4 + lax.rem(ep, 4))

    def zrecv(g):
        return remote(xs.at[src_plane(g)], X.at[src_plane(g), y, c], xsend.at[0, g], xrecv.at[0, g],
                      src_plane(g) * 4 + lax.rem(ep, 4))

    def ysend(g):
        s = src_plane(g)
        return remote(X.at[s, y, c], X.at[s, y, c], xsend.at[1, g], xrecv.at[1, g], e_y)

    def csend_a(g):
        s = src_plane(g)
        return remote(X.at[s, y, c], X.at[s, y, c], xsend.at[2, g], xrecv.at[2, g], e_core)

    def csend_b(g):
        s = src_plane(g)
        return remote(X.at[s, 1 - y, c], X.at[s, 1 - y, c], xsend.at[3, g], xrecv.at[3, g], e_core)

    def psend(g):
        return remote(ps.at[g], pr.at[g], xsend.at[4, g], xrecv.at[4, g], e_core)

    def rsend(g):
        return remote(ys.at[g], yr.at[g], xsend.at[5, g], xrecv.at[5, g], e_y)

    def bsend(g):
        return remote(zs.at[g], ret.at[z], xsend.at[6, g], xrecv.at[6, g],
                      src_plane(g) * 4 + lax.rem(ep, 4))

    def pack(i, carry):
        g = lax.rem(i + 1, T)
        d = dst_plane(g)
        o = pl.ds(pl.multiple_of(d * R, 16), R)
        blk = dot(pw[2, o, :], stk[...]).astype(BF)

        @pl.when(i < T - 1)
        def _():
            xs[d] = blk
            zsend(g).start()

        @pl.when(i == T - 1)
        def _():
            X[z, y, c] = blk

        return carry

    lax.fori_loop(0, T, pack, 0)
    for w in wcopies:
        w.wait()

    n0, n1 = HI, R - LO
    m0 = lax.broadcasted_iota(jnp.int32, (2, n0, HS), 1).reshape(2 * n0, HS) < 2 * CAP
    m1 = lax.broadcasted_iota(jnp.int32, (2, n1, HS), 1).reshape(2 * n1, HS) >= 2 * CAP - LO

    def hidden_of(s, a):
        lo, n, m = ((0, n0, m0), (LO, n1, m1))[a]
        acc = None
        for h in range(2):
            x = X[s, :, h, lo:lo + n, :].reshape(2 * n, H)
            v = dot(x, wg[a, h])
            acc = v if acc is None else acc + v
        gt, up = acc[:, :HS], acc[:, HS:]
        hid = gt / (1.0 + jnp.exp(-gt)) * up
        return jnp.where(m, hid, 0.0).astype(BF)

    def down(h0, h1, hh, store):
        o0 = dot(h0, wd[0, hh]).reshape(2, n0, H)
        o1 = dot(h1, wd[1, hh]).reshape(2, n1, H)
        if LO > 0:
            store(0, LO, o0[:, :LO])
        if HI > LO:
            store(LO, HI, o0[:, LO:] + o1[:, :HI - LO])
        if R > HI:
            store(HI, R, o1[:, HI - LO:])

    def step(k, carry):
        @pl.when(k < T)
        def _():
            @pl.when(k > 0)
            def _():
                zrecv(k).wait_recv()
            ysend(k).start()
            csend_a(k).start()

        @pl.when((k >= 1) & (k < T + 1))
        def _():
            g = k - 1
            s = src_plane(g)
            remote(X.at[s, 1 - y, c], X.at[s, 1 - y, c], xsend.at[1, g], xrecv.at[1, g], e_y).wait_recv()
            csend_b(g).start()

        @pl.when((k >= 1) & (k < T + 1))
        def _():
            g = k - 1
            s = src_plane(g)
            remote(X.at[s, y, 1 - c], X.at[s, y, 1 - c], xsend.at[2, g], xrecv.at[2, g], e_core).wait_recv()
            remote(X.at[s, 1 - y, 1 - c], X.at[s, 1 - y, 1 - c], xsend.at[3, g], xrecv.at[3, g],
                   e_core).wait_recv()
            h0 = hidden_of(s, 0)
            h1 = hidden_of(s, 1)

            def put(lo, hi, v):
                ps[g, :, lo:hi, :] = v.astype(BF)

            def keep(lo, hi, v):
                own[lax.rem(g, 2), :, lo:hi, :] = v

            down(h0, h1, 1 - c, put)
            psend(g).start()
            down(h0, h1, c, keep)

        @pl.when((k >= 2) & (k < T + 2))
        def _():
            g = k - 2
            psend(g).wait_recv()
            b = lax.rem(g, 2)
            ys[g] = (own[b, 1 - y] + pr[g, 1 - y].astype(F32)).astype(BF)
            rsend(g).start()
            ks[b] = own[b, y] + pr[g, y].astype(F32)

        @pl.when(k >= 3)
        def _():
            g = k - 3
            b = lax.rem(g, 2)
            rsend(g).wait_recv()
            v = (ks[b] + yr[g].astype(F32)).astype(BF)

            @pl.when(g > 0)
            def _():
                zs[g] = v
                bsend(g).start()

            @pl.when(g == 0)
            def _():
                ret[z] = v

        return carry

    lax.fori_loop(0, T + 3, step, 0)

    def got(g, carry):
        d = dst_plane(g)
        remote(zs.at[g], ret.at[d], xsend.at[6, g], xrecv.at[6, g], d * 4 + lax.rem(ep, 4)).wait_recv()
        return carry

    lax.fori_loop(1, T, got, 0)

    back = ret[...].reshape(T * R, H)
    w1 = pw[0].astype(F32).T.astype(BF)
    w2 = pw[1].astype(F32).T.astype(BF)
    fin[...] = (dot(w1, back) + dot(w2, back)).astype(BF)
    orow = pl.ds(pl.multiple_of((1 - c) * TOK, 16), TOK)
    fcopy = remote(fin.at[orow, :], out_ref.at[:, half(c)], tsend.at[2], trecv.at[2], e_core)
    fcopy.start()
    fl = pltpu.make_async_copy(fin.at[mrow, :], out_ref.at[:, half(c)], lsem.at[1])
    fl.start()

    def drain(g, carry):
        @pl.when(g > 0)
        def _():
            zsend(g).wait_send()
            bsend(g).wait_send()
        ysend(g).wait_send()
        csend_a(g).wait_send()
        csend_b(g).wait_send()
        psend(g).wait_send()
        rsend(g).wait_send()
        return carry

    lax.fori_loop(0, T, drain, 0)
    tcopy.wait_send()
    mcopy.wait_send()
    fl.wait()
    fcopy.wait_send()
    remote(fin.at[orow, :], out_ref.at[:, half(1 - c)], tsend.at[2], trecv.at[2], e_core).wait_recv()


def solution(mesh):
    devices = mesh.shape["ep"]
    T = devices // 4

    def local(tokens, w_gate_up, w_down, w_copy_gate_up, w_copy_down, routes, gate_weights, counts):
        tok, d = tokens.shape
        hs = w_down.shape[1]
        cap = 5 * tok * routes.shape[1] // (8 * T)
        R = -(-4 * cap // 16) * 16
        lo = 2 * cap // 16 * 16
        hi = -(-2 * cap // 16) * 16
        h = d // 2
        vm = pl.BlockSpec(memory_space=pltpu.VMEM)
        anym = pl.BlockSpec(memory_space=pl.ANY)
        return pl.pallas_call(
            functools.partial(kernel, T, cap, R, lo, hi),
            out_shape=jax.ShapeDtypeStruct((tok, d), BF),
            in_specs=[vm, anym, anym, anym, anym, vm, vm, pl.BlockSpec(memory_space=pltpu.SMEM)],
            out_specs=vm,
            scratch_shapes=[
                pltpu.VMEM((2, 2, h, 2 * hs), BF),
                pltpu.VMEM((2, 2, hs, h), BF),
                pltpu.VMEM((2 * tok, h), BF),
                pltpu.VMEM((2 * tok, 128), F32),
                pltpu.VMEM((T, R, h), BF),
                pltpu.VMEM((T, 2, 2, R, h), BF),
                pltpu.VMEM((3, T * R, 128), BF),
                pltpu.VMEM((T, 2, R, h), BF),
                pltpu.VMEM((T, 2, R, h), BF),
                pltpu.VMEM((2, 2, R, h), F32),
                pltpu.VMEM((T, R, h), BF),
                pltpu.VMEM((T, R, h), BF),
                pltpu.VMEM((2, R, h), F32),
                pltpu.VMEM((T, R, h), BF),
                pltpu.VMEM((T, R, h), BF),
                pltpu.VMEM((2 * tok, h), BF),
                pltpu.SemaphoreType.DMA((2,)),
                pltpu.SemaphoreType.DMA((8,)),
                pltpu.SemaphoreType.DMA((7, T)),
                pltpu.SemaphoreType.DMA((7, T)),
                pltpu.SemaphoreType.DMA((3,)),
                pltpu.SemaphoreType.DMA((3,)),
                pltpu.SemaphoreType.DMA((1,)),
            ],
            compiler_params=pltpu.CompilerParams(
                collective_id=0, has_side_effects=True, vmem_limit_bytes=60 * 1024 * 1024
            ),
        )(tokens, w_gate_up, w_down, w_copy_gate_up, w_copy_down, routes, gate_weights, counts)

    return jax.shard_map(
        local,
        mesh=mesh,
        in_specs=(
            P(("groups", "ep"), None),
            P("ep", None, None),
            P("ep", None, None),
            P("ep", None, None),
            P("ep", None, None),
            P(("groups", "ep"), None),
            P(("groups", "ep"), None),
            P(("groups", "ep")),
        ),
        out_specs=P(("groups", "ep"), None),
        check_vma=False,
    )
```

```python
import functools

import jax
import jax.numpy as jnp
from jax import lax
from jax.experimental import pallas as pl
from jax.experimental.pallas import tpu as pltpu
from jax.sharding import PartitionSpec as P

MESH = pl.DeviceIdType.MESH
BF = jnp.bfloat16
F32 = jnp.float32


def dot(a, b):
    return jnp.dot(a, b, preferred_element_type=F32)


def kernel(
    T, CAP, R, LO, HI, NC,
    tok_ref, wg_ref, wd_ref, cg_ref, cd_ref, rt_ref, gw_ref, cnt_ref,
    out_ref,
    wg, wd, stk, gm, xs, X, pw, ps, pr, own, ys, yr, ks, zs, ret, fin,
    lsem, wsem, xsend, xrecv, tsend, trecv,
):
    TOK = tok_ref.shape[0]
    TR = T * R
    D = tok_ref.shape[1]
    H = D // 2
    HC = H // NC
    HS = wd.shape[3]
    ep = lax.axis_index("ep")
    z = ep // 4
    y = (ep // 2) % 2
    c = ep % 2
    e_core = ep + 1 - 2 * c
    e_y = ep + 2 - 4 * y

    def src_plane(g):
        return lax.rem(z + g, T)

    def dst_plane(g):
        return lax.rem(z + T - g, T)

    def remote(src, dst, ssem, rsem, dev):
        return pltpu.make_async_remote_copy(
            src_ref=src, dst_ref=dst, send_sem=ssem, recv_sem=rsem,
            device_id={"ep": dev}, device_id_type=MESH,
        )

    def half(i):
        return pl.ds(pl.multiple_of(i * H, 128), H)

    wcopies = []
    for a, (gr, dr) in enumerate(((wg_ref, wd_ref), (cg_ref, cd_ref))):
        wcopies.append(pltpu.make_async_copy(gr.at[0], wg.at[a], wsem.at[0, a]))
        for h in range(2):
            for j in range(NC):
                wcopies.append(pltpu.make_async_copy(
                    dr.at[0, :, pl.ds(h * H + j * HC, HC)], wd.at[a, h, j], wsem.at[1 + h, a * NC + j]))
    rows = pl.ds(pl.multiple_of(c * TOK, 16), TOK)
    lcopy = pltpu.make_async_copy(tok_ref.at[:, half(c)], stk.at[rows, :], lsem.at[0])
    lcopy.start()

    barrier = pltpu.get_barrier_semaphore()
    for g in range(1, T):
        pl.semaphore_signal(barrier, inc=1, device_id={"ep": lax.rem(z + g, T) * 4 + lax.rem(ep, 4)},
                            device_id_type=MESH)
    pl.semaphore_signal(barrier, inc=1, device_id={"ep": e_core}, device_id_type=MESH)
    pl.semaphore_signal(barrier, inc=1, device_id={"ep": e_y}, device_id_type=MESH)

    n2 = 2 * TOK
    lane = lax.broadcasted_iota(jnp.int32, (128, n2), 1)
    row = lax.broadcasted_iota(jnp.int32, (128, n2), 0)
    off = lane - c * TOK
    live = (off >= 0) & (off < cnt_ref[0])
    twice = lambda v: jnp.broadcast_to(jnp.concatenate([v, v], axis=1), (128, n2))
    r0, r1 = twice(rt_ref[0:1, :]), twice(rt_ref[1:2, :])
    g0, g1 = twice(gw_ref[0:1, :]), twice(gw_ref[1:2, :])
    member = (row == r0) | (row == r1)
    gate = jnp.where(row == r0 + 64, g0, jnp.where(row == r1 + 64, g1, 0.0))
    gm[c] = jnp.where(live, jnp.where(member, 1.0, gate), 0.0)
    mrow = pl.ds(pl.multiple_of(c * TOK, 16), TOK)

    pl.semaphore_wait(barrier, T + 1)

    tcopy = remote(tok_ref.at[:, half(1 - c)], stk.at[rows, :], tsend.at[0], trecv.at[0], e_core)
    mcopy = remote(gm.at[c], gm.at[c], tsend.at[1], trecv.at[1], e_core)
    mcopy.start()
    tcopy.start()
    for w in wcopies:
        w.start()

    p = lax.broadcasted_iota(jnp.int32, (T, R, 128), 1).reshape(T * R, 128)
    team = lax.broadcasted_iota(jnp.int32, (T, R, 128), 0).reshape(T * R, 128)
    ln = lax.broadcasted_iota(jnp.int32, (T * R, 128), 1)
    one = lambda m: jnp.where(m, 1, 0)
    q = one(p >= CAP) + one(p >= 2 * CAP) + one(p >= 3 * CAP)
    copy_i = one(p >= 2 * CAP)
    core_i = q - 2 * copy_i
    rank_i = p - q * CAP
    valid = p < 4 * CAP
    inst = copy_i * T + team
    sel = jnp.where((ln == inst) & valid, 1.0, 0.0).astype(BF)
    selg = jnp.where((ln == inst + 64) & valid, 1.0, 0.0).astype(BF)
    tcore = one(ln >= TOK)
    ta = lax.broadcasted_iota(jnp.int32, (n2, n2), 0)
    tb = lax.broadcasted_iota(jnp.int32, (n2, n2), 1)
    low = jnp.where((ta < tb) & ((tb >= TOK) == (ta >= TOK)), 1.0, 0.0).astype(BF)

    mcopy.wait_recv()
    gall = gm[0] + gm[1]
    ghi = gall.astype(BF)
    glo = (gall - ghi.astype(F32)).astype(BF)
    rank = dot(ghi, low)
    a_m = dot(sel, ghi)
    a_r = dot(sel, rank.astype(BF))
    pick = (a_m > 0.5) & (a_r == rank_i.astype(F32)) & (tcore == core_i)
    pick = jnp.where(pick, 1.0, 0.0)
    pw[0] = (pick * dot(selg, ghi)).astype(BF)
    pw[1] = (pick * dot(selg, glo)).astype(BF)
    pw[2] = pick.astype(BF)
    lcopy.wait()
    tcopy.wait_recv()

    def zsend(g, j):
        return remote(xs.at[dst_plane(g), j], X.at[z, y, c, j], xsend.at[0, g, j], xrecv.at[0, g, j],
                      dst_plane(g) * 4 + lax.rem(ep, 4))

    def zrecv(g, j):
        s = src_plane(g)
        return remote(xs.at[s, j], X.at[s, y, c, j], xsend.at[0, g, j], xrecv.at[0, g, j], s * 4 + lax.rem(ep, 4))

    def xcopy(n, s, yy, cc, g, j, dev):
        r = X.at[s, yy, cc, j]
        return remote(r, r, xsend.at[n, g, j], xrecv.at[n, g, j], dev)

    def ysend(g, j):
        return xcopy(1, src_plane(g), y, c, g, j, e_y)

    def csend_a(g, j):
        return xcopy(2, src_plane(g), y, c, g, j, e_core)

    def csend_b(g, j):
        return xcopy(3, src_plane(g), 1 - y, c, g, j, e_core)

    def psend(g, j):
        return remote(ps.at[g, j], pr.at[g, j], xsend.at[4, g, j], xrecv.at[4, g, j], e_core)

    def rsend(g, j):
        return remote(ys.at[g, j], yr.at[g, j], xsend.at[5, g, j], xrecv.at[5, g, j], e_y)

    def bsend(g, j):
        return remote(zs.at[g, j], ret.at[j, z], xsend.at[6, g, j], xrecv.at[6, g, j],
                      src_plane(g) * 4 + lax.rem(ep, 4))

    def pack(i, carry):
        g = lax.rem(i + 1, T)
        d = dst_plane(g)
        o = pl.ds(pl.multiple_of(d * R, 16), R)
        for j in range(NC):
            blk = dot(pw[2, o, :], stk[:, j * HC:(j + 1) * HC]).astype(BF)

            @pl.when(i < T - 1)
            def _():
                xs[d, j] = blk
                zsend(g, j).start()

            @pl.when(i == T - 1)
            def _():
                X[z, y, c, j] = blk
                ysend(0, j).start()
                csend_a(0, j).start()

        return carry

    lax.fori_loop(0, T, pack, 0)

    n0, n1 = HI, R - LO
    m0 = lax.broadcasted_iota(jnp.int32, (2, n0, HS), 1).reshape(2 * n0, HS) < 2 * CAP
    m1 = lax.broadcasted_iota(jnp.int32, (2, n1, HS), 1).reshape(2 * n1, HS) >= 2 * CAP - LO

    def hidden_of(s, a):
        lo, n, m = ((0, n0, m0), (LO, n1, m1))[a]
        acc = None
        for h in range(2):
            for j in range(NC):
                x = X[s, :, h, j, lo:lo + n, :].reshape(2 * n, HC)
                v = dot(x, wg[a, h * H + j * HC:h * H + (j + 1) * HC, :])
                acc = v if acc is None else acc + v
        gt, up = acc[:, :HS], acc[:, HS:]
        hid = gt / (1.0 + jnp.exp(-gt)) * up
        return jnp.where(m, hid, 0.0).astype(BF)

    def down(h0, h1, hh, j, store):
        o0 = dot(h0, wd[0, hh, j]).reshape(2, n0, HC)
        o1 = dot(h1, wd[1, hh, j]).reshape(2, n1, HC)
        if LO > 0:
            store(0, LO, o0[:, :LO])
        if HI > LO:
            store(LO, HI, o0[:, LO:] + o1[:, :HI - LO])
        if R > HI:
            store(HI, R, o1[:, HI - LO:])

    def step(k, carry):
        @pl.when((k > 0) & (k < T))
        def _():
            for j in range(NC):
                zrecv(k, j).wait_recv()
                ysend(k, j).start()
                csend_a(k, j).start()

        @pl.when((k >= 1) & (k < T + 1))
        def _():
            g = k - 1
            s = src_plane(g)
            for j in range(NC):
                xcopy(1, s, 1 - y, c, g, j, e_y).wait_recv()
                csend_b(g, j).start()

            @pl.when(k == 1)
            def _():
                for w in wcopies:
                    w.wait()

            for j in range(NC):
                xcopy(2, s, y, 1 - c, g, j, e_core).wait_recv()
                xcopy(3, s, 1 - y, 1 - c, g, j, e_core).wait_recv()
            h0 = hidden_of(s, 0)
            h1 = hidden_of(s, 1)
            for j in range(NC):
                def put(lo, hi, v, j=j):
                    ps[g, j, :, lo:hi, :] = v.astype(BF)

                down(h0, h1, 1 - c, j, put)
                psend(g, j).start()
            for j in range(NC):
                def keep(lo, hi, v, j=j):
                    own[j, :, lo:hi, :] = v

                down(h0, h1, c, j, keep)

        @pl.when(k >= 2)
        def _():
            g = k - 2
            for j in range(NC):
                rsend(g, j).wait_recv()
                v = (ks[j] + yr[g, j].astype(F32)).astype(BF)

                @pl.when(g > 0)
                def _():
                    zs[g, j] = v
                    bsend(g, j).start()

                @pl.when(g == 0)
                def _():
                    ret[j, z] = v

        @pl.when((k >= 1) & (k < T + 1))
        def _():
            g = k - 1
            for j in range(NC):
                psend(g, j).wait_recv()
                ys[g, j] = (own[j, 1 - y] + pr[g, j, 1 - y].astype(F32)).astype(BF)
                rsend(g, j).start()
                ks[j] = own[j, y] + pr[g, j, y].astype(F32)

        return carry

    lax.fori_loop(0, T + 2, step, 0)

    w1 = pw[0].astype(F32).T.astype(BF)
    w2 = pw[1].astype(F32).T.astype(BF)
    orow = pl.ds(pl.multiple_of((1 - c) * TOK, 16), TOK)
    fl = []
    fc = []
    for j in range(NC):
        def got(g, carry, j=j):
            d = dst_plane(g)
            remote(zs.at[g, j], ret.at[j, d], xsend.at[6, g, j], xrecv.at[6, g, j],
                   d * 4 + lax.rem(ep, 4)).wait_recv()
            return carry

        lax.fori_loop(1, T, got, 0)
        back = ret[j].reshape(TR, HC)
        fin[j] = (dot(w1, back) + dot(w2, back)).astype(BF)

        def cols(i, j=j):
            return pl.ds(pl.multiple_of(i * H + j * HC, 128), HC)

        fc.append(remote(fin.at[j, orow, :], out_ref.at[:, cols(c)], tsend.at[2 + j], trecv.at[2 + j], e_core))
        fc[-1].start()
        fl.append(pltpu.make_async_copy(fin.at[j, mrow, :], out_ref.at[:, cols(c)], lsem.at[1 + j]))
        fl[-1].start()

    def drain(g, carry):
        for j in range(NC):
            @pl.when(g > 0)
            def _():
                zsend(g, j).wait_send()
                bsend(g, j).wait_send()
            ysend(g, j).wait_send()
            csend_a(g, j).wait_send()
            csend_b(g, j).wait_send()
            psend(g, j).wait_send()
            rsend(g, j).wait_send()
        return carry

    lax.fori_loop(0, T, drain, 0)
    tcopy.wait_send()
    mcopy.wait_send()
    for j in range(NC):
        fl[j].wait()
        fc[j].wait_send()
        cc = pl.ds(pl.multiple_of((1 - c) * H + j * HC, 128), HC)
        remote(fin.at[j, orow, :], out_ref.at[:, cc], tsend.at[2 + j], trecv.at[2 + j], e_core).wait_recv()


NC = 2


def solution(mesh):
    devices = mesh.shape["ep"]
    T = devices // 4

    def local(tokens, w_gate_up, w_down, w_copy_gate_up, w_copy_down, routes, gate_weights, counts):
        tok, d = tokens.shape
        hs = w_down.shape[1]
        cap = 5 * tok * routes.shape[1] // (8 * T)
        R = -(-4 * cap // 16) * 16
        lo = 2 * cap // 16 * 16
        hi = -(-2 * cap // 16) * 16
        h = d // 2
        hc = h // NC
        vm = pl.BlockSpec(memory_space=pltpu.VMEM)
        anym = pl.BlockSpec(memory_space=pl.ANY)
        return pl.pallas_call(
            functools.partial(kernel, T, cap, R, lo, hi, NC),
            out_shape=jax.ShapeDtypeStruct((tok, d), BF),
            in_specs=[anym, anym, anym, anym, anym, vm, vm, pl.BlockSpec(memory_space=pltpu.SMEM)],
            out_specs=vm,
            scratch_shapes=[
                pltpu.VMEM((2, d, 2 * hs), BF),
                pltpu.VMEM((2, 2, NC, hs, hc), BF),
                pltpu.VMEM((2 * tok, h), BF),
                pltpu.VMEM((2, 128, 2 * tok), F32),
                pltpu.VMEM((T, NC, R, hc), BF),
                pltpu.VMEM((T, 2, 2, NC, R, hc), BF),
                pltpu.VMEM((3, T * R, 128), BF),
                pltpu.VMEM((T, NC, 2, R, hc), BF),
                pltpu.VMEM((T, NC, 2, R, hc), BF),
                pltpu.VMEM((NC, 2, R, hc), F32),
                pltpu.VMEM((T, NC, R, hc), BF),
                pltpu.VMEM((T, NC, R, hc), BF),
                pltpu.VMEM((NC, R, hc), F32),
                pltpu.VMEM((T, NC, R, hc), BF),
                pltpu.VMEM((NC, T, R, hc), BF),
                pltpu.VMEM((NC, 2 * tok, hc), BF),
                pltpu.SemaphoreType.DMA((1 + NC,)),
                pltpu.SemaphoreType.DMA((3, 2 * NC)),
                pltpu.SemaphoreType.DMA((7, T, NC)),
                pltpu.SemaphoreType.DMA((7, T, NC)),
                pltpu.SemaphoreType.DMA((2 + NC,)),
                pltpu.SemaphoreType.DMA((2 + NC,)),
            ],
            compiler_params=pltpu.CompilerParams(
                collective_id=0, has_side_effects=True, vmem_limit_bytes=60 * 1024 * 1024
            ),
        )(tokens, w_gate_up, w_down, w_copy_gate_up, w_copy_down, routes.T, gate_weights.T, counts)

    return jax.shard_map(
        local,
        mesh=mesh,
        in_specs=(
            P(("groups", "ep"), None),
            P("ep", None, None),
            P("ep", None, None),
            P("ep", None, None),
            P("ep", None, None),
            P(("groups", "ep"), None),
            P(("groups", "ep"), None),
            P(("groups", "ep")),
        ),
        out_specs=P(("groups", "ep"), None),
        check_vma=False,
    )
```

```python
import functools

import jax
import jax.numpy as jnp
from jax import lax
from jax.experimental import pallas as pl
from jax.experimental.pallas import tpu as pltpu
from jax.sharding import PartitionSpec as P

MESH = pl.DeviceIdType.MESH
BF = jnp.bfloat16
F32 = jnp.float32


def dot(a, b):
    return jnp.dot(a, b, preferred_element_type=F32)


def kernel(
    T, CAP, R, LO, HI, NC,
    tok_ref, wg_ref, wd_ref, cg_ref, cd_ref, rt_ref, gw_ref, cnt_ref,
    out_ref,
    wg, wd, stk, gm, xs, X, pw, ps, pr, own, ys, yr, ks, zs, ret, fin, wt,
    lsem, wsem, xsend, xrecv, tsend, trecv,
):
    TOK = tok_ref.shape[0]
    TR = T * R
    D = tok_ref.shape[1]
    H = D // 2
    HC = H // NC
    HS = wd.shape[3]
    ep = lax.axis_index("ep")
    z = ep // 4
    y = (ep // 2) % 2
    c = ep % 2
    e_core = ep + 1 - 2 * c
    e_y = ep + 2 - 4 * y

    def src_plane(g):
        return lax.rem(z + g, T)

    def dst_plane(g):
        return lax.rem(z + T - g, T)

    def remote(src, dst, ssem, rsem, dev):
        return pltpu.make_async_remote_copy(
            src_ref=src, dst_ref=dst, send_sem=ssem, recv_sem=rsem,
            device_id={"ep": dev}, device_id_type=MESH,
        )

    def half(i):
        return pl.ds(pl.multiple_of(i * H, 128), H)

    wcopies = []
    for a, (gr, dr) in enumerate(((wg_ref, wd_ref), (cg_ref, cd_ref))):
        wcopies.append(pltpu.make_async_copy(gr.at[0], wg.at[a], wsem.at[0, a]))
        for h in range(2):
            for j in range(NC):
                wcopies.append(pltpu.make_async_copy(
                    dr.at[0, :, pl.ds(h * H + j * HC, HC)], wd.at[a, h, j], wsem.at[1 + h, a * NC + j]))
    rows = pl.ds(pl.multiple_of(c * TOK, 16), TOK)
    lcopy = pltpu.make_async_copy(tok_ref.at[:, half(c)], stk.at[rows, :], lsem.at[0])
    lcopy.start()

    barrier = pltpu.get_barrier_semaphore()
    for g in range(1, T):
        pl.semaphore_signal(barrier, inc=1, device_id={"ep": lax.rem(z + g, T) * 4 + lax.rem(ep, 4)},
                            device_id_type=MESH)
    pl.semaphore_signal(barrier, inc=1, device_id={"ep": e_core}, device_id_type=MESH)
    pl.semaphore_signal(barrier, inc=1, device_id={"ep": e_y}, device_id_type=MESH)

    n2 = 2 * TOK
    lane = lax.broadcasted_iota(jnp.int32, (128, n2), 1)
    row = lax.broadcasted_iota(jnp.int32, (128, n2), 0)
    off = lane - c * TOK
    live = (off >= 0) & (off < cnt_ref[0])
    twice = lambda v: jnp.broadcast_to(jnp.concatenate([v, v], axis=1), (128, n2))
    r0, r1 = twice(rt_ref[0:1, :]), twice(rt_ref[1:2, :])
    g0, g1 = twice(gw_ref[0:1, :]), twice(gw_ref[1:2, :])
    member = (row == r0) | (row == r1)
    gate = jnp.where(row == r0 + 64, g0, jnp.where(row == r1 + 64, g1, 0.0))
    gm[c] = jnp.where(live, jnp.where(member, 1.0, gate), 0.0)
    mrow = pl.ds(pl.multiple_of(c * TOK, 16), TOK)

    pl.semaphore_wait(barrier, T + 1)

    tcopy = remote(tok_ref.at[:, half(1 - c)], stk.at[rows, :], tsend.at[0], trecv.at[0], e_core)
    mcopy = remote(gm.at[c], gm.at[c], tsend.at[1], trecv.at[1], e_core)
    mcopy.start()
    tcopy.start()

    p = lax.broadcasted_iota(jnp.int32, (T, R, 128), 1).reshape(T * R, 128)
    team = lax.broadcasted_iota(jnp.int32, (T, R, 128), 0).reshape(T * R, 128)
    ln = lax.broadcasted_iota(jnp.int32, (T * R, 128), 1)
    one = lambda m: jnp.where(m, 1, 0)
    q = one(p >= CAP) + one(p >= 2 * CAP) + one(p >= 3 * CAP)
    copy_i = one(p >= 2 * CAP)
    core_i = q - 2 * copy_i
    rank_i = p - q * CAP
    valid = p < 4 * CAP
    inst = copy_i * T + team
    sel = jnp.where((ln == inst) & valid, 1.0, 0.0).astype(BF)
    selg = jnp.where((ln == inst + 64) & valid, 1.0, 0.0).astype(BF)
    tcore = one(ln >= TOK)
    ta = lax.broadcasted_iota(jnp.int32, (n2, n2), 0)
    tb = lax.broadcasted_iota(jnp.int32, (n2, n2), 1)
    low = jnp.where((ta < tb) & ((tb >= TOK) == (ta >= TOK)), 1.0, 0.0).astype(BF)

    mcopy.wait_recv()
    gall = gm[0] + gm[1]
    ghi = gall.astype(BF)
    glo = (gall - ghi.astype(F32)).astype(BF)
    rank = dot(ghi, low)
    a_m = dot(sel, ghi)
    a_r = dot(sel, rank.astype(BF))
    pick = (a_m > 0.5) & (a_r == rank_i.astype(F32)) & (tcore == core_i)
    pick = jnp.where(pick, 1.0, 0.0)
    pw[0] = (pick * dot(selg, ghi)).astype(BF)
    pw[1] = (pick * dot(selg, glo)).astype(BF)
    pw[2] = pick.astype(BF)
    lcopy.wait()
    tcopy.wait_recv()
    for w in wcopies:
        w.start()

    def zsend(g, j):
        return remote(xs.at[dst_plane(g), j], X.at[z, y, c, j], xsend.at[0, g, j], xrecv.at[0, g, j],
                      dst_plane(g) * 4 + lax.rem(ep, 4))

    def zrecv(g, j):
        s = src_plane(g)
        return remote(xs.at[s, j], X.at[s, y, c, j], xsend.at[0, g, j], xrecv.at[0, g, j], s * 4 + lax.rem(ep, 4))

    def xcopy(n, s, yy, cc, g, j, dev):
        r = X.at[s, yy, cc, j]
        return remote(r, r, xsend.at[n, g, j], xrecv.at[n, g, j], dev)

    def ysend(g, j):
        return xcopy(1, src_plane(g), y, c, g, j, e_y)

    def csend_a(g, j):
        return xcopy(2, src_plane(g), y, c, g, j, e_core)

    def csend_b(g, j):
        return xcopy(3, src_plane(g), 1 - y, c, g, j, e_core)

    def psend(g, j):
        return remote(ps.at[g, j], pr.at[g, j], xsend.at[4, g, j], xrecv.at[4, g, j], e_core)

    def rsend(g, j):
        return remote(ys.at[g, j], yr.at[g, j], xsend.at[5, g, j], xrecv.at[5, g, j], e_y)

    def bsend(g, j):
        return remote(zs.at[g, j], ret.at[j, z], xsend.at[6, g, j], xrecv.at[6, g, j],
                      src_plane(g) * 4 + lax.rem(ep, 4))

    def pack(i, carry):
        g = i
        d = dst_plane(g)
        o = pl.ds(pl.multiple_of(d * R, 16), R)
        for j in range(NC):
            blk = dot(pw[2, o, :], stk[:, j * HC:(j + 1) * HC]).astype(BF)

            @pl.when(i > 0)
            def _():
                xs[d, j] = blk

                @pl.when(g <= 1)
                def _():
                    zsend(g, j).start()

            @pl.when(i == 0)
            def _():
                X[z, y, c, j] = blk
                ysend(0, j).start()
                csend_a(0, j).start()

        return carry

    lax.fori_loop(0, T, pack, 0)

    wt[0] = pw[0].astype(F32).T.astype(BF)
    wt[1] = pw[1].astype(F32).T.astype(BF)
    n0, n1 = HI, R - LO
    m0 = lax.broadcasted_iota(jnp.int32, (2, n0, HS), 1).reshape(2 * n0, HS) < 2 * CAP
    m1 = lax.broadcasted_iota(jnp.int32, (2, n1, HS), 1).reshape(2 * n1, HS) >= 2 * CAP - LO

    spans = ((0, n0, m0), (LO, n1, m1))

    def up_part(s, hh, j, acc):
        at = pl.ds(pl.multiple_of(hh * H + j * HC, 128), HC)
        new = []
        for a, (lo, n, m) in enumerate(spans):
            x = X[s, :, hh, j, lo:lo + n, :].reshape(2 * n, HC)
            v = dot(x, wg[a, at, :])
            new.append(v if acc is None else acc[a] + v)
        return new

    def act(a, acc):
        gt, up = acc[:, :HS], acc[:, HS:]
        hid = gt / (1.0 + jnp.exp(-gt)) * up
        return jnp.where(spans[a][2], hid, 0.0).astype(BF)

    def down(h0, h1, hh, j, store):
        o0 = dot(h0, wd[0, hh, j]).reshape(2, n0, HC)
        o1 = dot(h1, wd[1, hh, j]).reshape(2, n1, HC)
        if LO > 0:
            store(0, LO, o0[:, :LO])
        if HI > LO:
            store(LO, HI, o0[:, LO:] + o1[:, :HI - LO])
        if R > HI:
            store(HI, R, o1[:, HI - LO:])

    def step(k, carry):
        @pl.when((k > 0) & (k < T))
        def _():
            for j in range(NC):
                zrecv(k, j).wait_recv()
                ysend(k, j).start()
                csend_a(k, j).start()

                @pl.when(k + 1 < T)
                def _():
                    zsend(k + 1, j).start()

        @pl.when((k >= 1) & (k < T + 1))
        def _():
            g = k - 1
            s = src_plane(g)
            for j in range(NC):
                xcopy(1, s, 1 - y, c, g, j, e_y).wait_recv()
                csend_b(g, j).start()

            @pl.when(k == 1)
            def _():
                for w in wcopies:
                    w.wait()

            acc = None
            for j in range(NC):
                acc = up_part(s, c, j, acc)
            for j in range(NC):
                xcopy(2, s, y, 1 - c, g, j, e_core).wait_recv()
                xcopy(3, s, 1 - y, 1 - c, g, j, e_core).wait_recv()
                acc = up_part(s, 1 - c, j, acc)
            h0 = act(0, acc[0])
            h1 = act(1, acc[1])
            for j in range(NC):
                def put(lo, hi, v, j=j):
                    ps[g, j, :, lo:hi, :] = v.astype(BF)

                down(h0, h1, 1 - c, j, put)
                psend(g, j).start()
            for j in range(NC):
                def keep(lo, hi, v, j=j):
                    own[j, :, lo:hi, :] = v

                down(h0, h1, c, j, keep)

        @pl.when(k >= 2)
        def _():
            g = k - 2
            for j in range(NC):
                rsend(g, j).wait_recv()
                v = (ks[j] + yr[g, j].astype(F32)).astype(BF)

                @pl.when(g > 0)
                def _():
                    zs[g, j] = v
                    bsend(g, j).start()

                @pl.when(g == 0)
                def _():
                    ret[j, z] = v

        @pl.when((k >= 1) & (k < T + 1))
        def _():
            g = k - 1
            for j in range(NC):
                psend(g, j).wait_recv()
                ys[g, j] = (own[j, 1 - y] + pr[g, j, 1 - y].astype(F32)).astype(BF)
                rsend(g, j).start()
                ks[j] = own[j, y] + pr[g, j, y].astype(F32)

        return carry

    lax.fori_loop(0, T + 2, step, 0)

    orow = pl.ds(pl.multiple_of((1 - c) * TOK, 16), TOK)
    fl = []
    fc = []
    for j in range(NC):
        def got(g, carry, j=j):
            d = dst_plane(g)
            remote(zs.at[g, j], ret.at[j, d], xsend.at[6, g, j], xrecv.at[6, g, j],
                   d * 4 + lax.rem(ep, 4)).wait_recv()
            return carry

        lax.fori_loop(1, T, got, 0)
        back = ret[j].reshape(TR, HC)
        fin[j] = (dot(wt[0], back) + dot(wt[1], back)).astype(BF)

        def cols(i, j=j):
            return pl.ds(pl.multiple_of(i * H + j * HC, 128), HC)

        fc.append(remote(fin.at[j, orow, :], out_ref.at[:, cols(c)], tsend.at[2 + j], trecv.at[2 + j], e_core))
        fc[-1].start()
        fl.append(pltpu.make_async_copy(fin.at[j, mrow, :], out_ref.at[:, cols(c)], lsem.at[1 + j]))
        fl[-1].start()

    def drain(g, carry):
        for j in range(NC):
            @pl.when(g > 0)
            def _():
                zsend(g, j).wait_send()
                bsend(g, j).wait_send()
            ysend(g, j).wait_send()
            csend_a(g, j).wait_send()
            csend_b(g, j).wait_send()
            psend(g, j).wait_send()
            rsend(g, j).wait_send()
        return carry

    lax.fori_loop(0, T, drain, 0)
    tcopy.wait_send()
    mcopy.wait_send()
    for j in range(NC):
        fl[j].wait()
        fc[j].wait_send()
        cc = pl.ds(pl.multiple_of((1 - c) * H + j * HC, 128), HC)
        remote(fin.at[j, orow, :], out_ref.at[:, cc], tsend.at[2 + j], trecv.at[2 + j], e_core).wait_recv()


NC = 2


def solution(mesh):
    devices = mesh.shape["ep"]
    T = devices // 4

    def local(tokens, w_gate_up, w_down, w_copy_gate_up, w_copy_down, routes, gate_weights, counts):
        tok, d = tokens.shape
        hs = w_down.shape[1]
        cap = 5 * tok * routes.shape[1] // (8 * T)
        R = -(-4 * cap // 16) * 16
        lo = 2 * cap // 16 * 16
        hi = -(-2 * cap // 16) * 16
        h = d // 2
        hc = h // NC
        vm = pl.BlockSpec(memory_space=pltpu.VMEM)
        anym = pl.BlockSpec(memory_space=pl.ANY)
        return pl.pallas_call(
            functools.partial(kernel, T, cap, R, lo, hi, NC),
            out_shape=jax.ShapeDtypeStruct((tok, d), BF),
            in_specs=[anym, anym, anym, anym, anym, vm, vm, pl.BlockSpec(memory_space=pltpu.SMEM)],
            out_specs=anym,
            scratch_shapes=[
                pltpu.VMEM((2, d, 2 * hs), BF),
                pltpu.VMEM((2, 2, NC, hs, hc), BF),
                pltpu.VMEM((2 * tok, h), BF),
                pltpu.VMEM((2, 128, 2 * tok), F32),
                pltpu.VMEM((T, NC, R, hc), BF),
                pltpu.VMEM((T, 2, 2, NC, R, hc), BF),
                pltpu.VMEM((3, T * R, 128), BF),
                pltpu.VMEM((T, NC, 2, R, hc), BF),
                pltpu.VMEM((T, NC, 2, R, hc), BF),
                pltpu.VMEM((NC, 2, R, hc), F32),
                pltpu.VMEM((T, NC, R, hc), BF),
                pltpu.VMEM((T, NC, R, hc), BF),
                pltpu.VMEM((NC, R, hc), F32),
                pltpu.VMEM((T, NC, R, hc), BF),
                pltpu.VMEM((NC, T, R, hc), BF),
                pltpu.VMEM((NC, 2 * tok, hc), BF),
                pltpu.VMEM((2, 2 * tok, T * R), BF),
                pltpu.SemaphoreType.DMA((1 + NC,)),
                pltpu.SemaphoreType.DMA((3, 2 * NC)),
                pltpu.SemaphoreType.DMA((7, T, NC)),
                pltpu.SemaphoreType.DMA((7, T, NC)),
                pltpu.SemaphoreType.DMA((2 + NC,)),
                pltpu.SemaphoreType.DMA((2 + NC,)),
            ],
            compiler_params=pltpu.CompilerParams(
                collective_id=0, has_side_effects=True, vmem_limit_bytes=60 * 1024 * 1024
            ),
        )(tokens, w_gate_up, w_down, w_copy_gate_up, w_copy_down, routes.T, gate_weights.T, counts)

    return jax.shard_map(
        local,
        mesh=mesh,
        in_specs=(
            P(("groups", "ep"), None),
            P("ep", None, None),
            P("ep", None, None),
            P("ep", None, None),
            P("ep", None, None),
            P(("groups", "ep"), None),
            P(("groups", "ep"), None),
            P(("groups", "ep")),
        ),
        out_specs=P(("groups", "ep"), None),
        check_vma=False,
    )
```

```python
import functools

import jax
import jax.numpy as jnp
from jax import lax
from jax.experimental import pallas as pl
from jax.experimental.pallas import tpu as pltpu
from jax.sharding import PartitionSpec as P

MESH = pl.DeviceIdType.MESH
BF = jnp.bfloat16
F32 = jnp.float32


def dot(a, b):
    return jnp.dot(a, b, preferred_element_type=F32)


def kernel(
    T, CAP, R, LO, HI, NC,
    tok_ref, wg_ref, wd_ref, cg_ref, cd_ref, rt_ref, gw_ref, cnt_ref,
    out_ref,
    wg, wd, stk, gm, xs, X, pw, ps, pr, own, ys, yr, ks, zs, ret, fin, wt,
    lsem, wsem, xsend, xrecv, tsend, trecv,
):
    TOK = tok_ref.shape[0]
    TR = T * R
    D = tok_ref.shape[1]
    H = D // 2
    HC = H // NC
    HS = wd.shape[3]
    ep = lax.axis_index("ep")
    z = ep // 4
    y = (ep // 2) % 2
    c = ep % 2
    e_core = ep + 1 - 2 * c
    e_y = ep + 2 - 4 * y

    def src_plane(g):
        return lax.rem(z + g, T)

    def dst_plane(g):
        return lax.rem(z + T - g, T)

    def remote(src, dst, ssem, rsem, dev):
        return pltpu.make_async_remote_copy(
            src_ref=src, dst_ref=dst, send_sem=ssem, recv_sem=rsem,
            device_id={"ep": dev}, device_id_type=MESH,
        )

    def half(i):
        return pl.ds(pl.multiple_of(i * H, 128), H)

    wcopies = []
    for a, (gr, dr) in enumerate(((wg_ref, wd_ref), (cg_ref, cd_ref))):
        wcopies.append(pltpu.make_async_copy(gr.at[0], wg.at[a], wsem.at[0, a]))
        for h in range(2):
            for j in range(NC):
                wcopies.append(pltpu.make_async_copy(
                    dr.at[0, :, pl.ds(h * H + j * HC, HC)], wd.at[a, h, j], wsem.at[1 + h, a * NC + j]))
    rows = pl.ds(pl.multiple_of(c * TOK, 16), TOK)
    lcopy = pltpu.make_async_copy(tok_ref.at[:, half(c)], stk.at[rows, :], lsem.at[0])
    lcopy.start()

    barrier = pltpu.get_barrier_semaphore()
    for g in range(1, T):
        pl.semaphore_signal(barrier, inc=1, device_id={"ep": lax.rem(z + g, T) * 4 + lax.rem(ep, 4)},
                            device_id_type=MESH)
    pl.semaphore_signal(barrier, inc=1, device_id={"ep": e_core}, device_id_type=MESH)
    pl.semaphore_signal(barrier, inc=1, device_id={"ep": e_y}, device_id_type=MESH)

    n2 = 2 * TOK
    lane = lax.broadcasted_iota(jnp.int32, (128, n2), 1)
    row = lax.broadcasted_iota(jnp.int32, (128, n2), 0)
    off = lane - c * TOK
    live = (off >= 0) & (off < cnt_ref[0])
    twice = lambda v: jnp.broadcast_to(jnp.concatenate([v, v], axis=1), (128, n2))
    r0, r1 = twice(rt_ref[0:1, :]), twice(rt_ref[1:2, :])
    g0, g1 = twice(gw_ref[0:1, :]), twice(gw_ref[1:2, :])
    member = (row == r0) | (row == r1)
    gate = jnp.where(row == r0 + 64, g0, jnp.where(row == r1 + 64, g1, 0.0))
    gm[c] = jnp.where(live, jnp.where(member, 1.0, gate), 0.0)
    mrow = pl.ds(pl.multiple_of(c * TOK, 16), TOK)

    pl.semaphore_wait(barrier, T + 1)

    tcopy = remote(tok_ref.at[:, half(1 - c)], stk.at[rows, :], tsend.at[0], trecv.at[0], e_core)
    mcopy = remote(gm.at[c], gm.at[c], tsend.at[1], trecv.at[1], e_core)
    mcopy.start()
    tcopy.start()

    p = lax.broadcasted_iota(jnp.int32, (T, R, 128), 1).reshape(T * R, 128)
    team = lax.broadcasted_iota(jnp.int32, (T, R, 128), 0).reshape(T * R, 128)
    ln = lax.broadcasted_iota(jnp.int32, (T * R, 128), 1)
    one = lambda m: jnp.where(m, 1, 0)
    q = one(p >= CAP) + one(p >= 2 * CAP) + one(p >= 3 * CAP)
    copy_i = one(p >= 2 * CAP)
    core_i = q - 2 * copy_i
    rank_i = p - q * CAP
    valid = p < 4 * CAP
    inst = copy_i * T + team
    sel = jnp.where((ln == inst) & valid, 1.0, 0.0).astype(BF)
    selg = jnp.where((ln == inst + 64) & valid, 1.0, 0.0).astype(BF)
    tcore = one(ln >= TOK)
    ta = lax.broadcasted_iota(jnp.int32, (n2, n2), 0)
    tb = lax.broadcasted_iota(jnp.int32, (n2, n2), 1)
    low = jnp.where((ta < tb) & ((tb >= TOK) == (ta >= TOK)), 1.0, 0.0).astype(BF)

    mcopy.wait_recv()
    gall = gm[0] + gm[1]
    ghi = gall.astype(BF)
    glo = (gall - ghi.astype(F32)).astype(BF)
    rank = dot(ghi, low)
    a_m = dot(sel, ghi)
    a_r = dot(sel, rank.astype(BF))
    pick = (a_m > 0.5) & (a_r == rank_i.astype(F32)) & (tcore == core_i)
    pick = jnp.where(pick, 1.0, 0.0)
    pw[0] = (pick * dot(selg, ghi)).astype(BF)
    pw[1] = (pick * dot(selg, glo)).astype(BF)
    pw[2] = pick.astype(BF)
    lcopy.wait()
    tcopy.wait_recv()
    for w in wcopies:
        w.start()

    def zsend(g, j):
        return remote(xs.at[dst_plane(g), j], X.at[z, y, c, j], xsend.at[0, g, j], xrecv.at[0, g, j],
                      dst_plane(g) * 4 + lax.rem(ep, 4))

    def zrecv(g, j):
        s = src_plane(g)
        return remote(xs.at[s, j], X.at[s, y, c, j], xsend.at[0, g, j], xrecv.at[0, g, j], s * 4 + lax.rem(ep, 4))

    def xcopy(n, s, yy, cc, g, j, dev):
        r = X.at[s, yy, cc, j]
        return remote(r, r, xsend.at[n, g, j], xrecv.at[n, g, j], dev)

    def ysend(g, j):
        return xcopy(1, src_plane(g), y, c, g, j, e_y)

    def csend_a(g, j):
        return xcopy(2, src_plane(g), y, c, g, j, e_core)

    def csend_b(g, j):
        return xcopy(3, src_plane(g), 1 - y, c, g, j, e_core)

    def psend(g, j):
        return remote(ps.at[g, j], pr.at[g, j], xsend.at[4, g, j], xrecv.at[4, g, j], e_core)

    def rsend(g, j):
        return remote(ys.at[g, j], yr.at[g, j], xsend.at[5, g, j], xrecv.at[5, g, j], e_y)

    def bsend(g, j):
        return remote(zs.at[g, j], ret.at[j, z], xsend.at[6, g, j], xrecv.at[6, g, j],
                      src_plane(g) * 4 + lax.rem(ep, 4))

    def pack(i, carry):
        g = i
        d = dst_plane(g)
        o = pl.ds(pl.multiple_of(d * R, 16), R)
        for j in range(NC):
            blk = dot(pw[2, o, :], stk[:, j * HC:(j + 1) * HC]).astype(BF)

            @pl.when(i > 0)
            def _():
                xs[d, j] = blk

                @pl.when(g <= 1)
                def _():
                    zsend(g, j).start()

            @pl.when(i == 0)
            def _():
                X[z, y, c, j] = blk
                ysend(0, j).start()
                csend_a(0, j).start()

        return carry

    lax.fori_loop(0, T, pack, 0)

    wt[0] = pw[0].astype(F32).T.astype(BF)
    wt[1] = pw[1].astype(F32).T.astype(BF)
    n0, n1 = HI, R - LO
    m0 = lax.broadcasted_iota(jnp.int32, (2, n0, HS), 1).reshape(2 * n0, HS) < 2 * CAP
    m1 = lax.broadcasted_iota(jnp.int32, (2, n1, HS), 1).reshape(2 * n1, HS) >= 2 * CAP - LO

    spans = ((0, n0, m0), (LO, n1, m1))

    def up_part(s, hh, j, acc):
        at = pl.ds(pl.multiple_of(hh * H + j * HC, 128), HC)
        new = []
        for a, (lo, n, m) in enumerate(spans):
            x = X[s, :, hh, j, lo:lo + n, :].reshape(2 * n, HC)
            v = dot(x, wg[a, at, :])
            new.append(v if acc is None else acc[a] + v)
        return new

    def act(a, acc):
        gt, up = acc[:, :HS], acc[:, HS:]
        hid = gt / (1.0 + jnp.exp(-gt)) * up
        return jnp.where(spans[a][2], hid, 0.0).astype(BF)

    def down(h0, h1, hh, j, store):
        o0 = dot(h0, wd[0, hh, j]).reshape(2, n0, HC)
        o1 = dot(h1, wd[1, hh, j]).reshape(2, n1, HC)
        if LO > 0:
            store(0, LO, o0[:, :LO])
        if HI > LO:
            store(LO, HI, o0[:, LO:] + o1[:, :HI - LO])
        if R > HI:
            store(HI, R, o1[:, HI - LO:])

    def step(k, carry):
        @pl.when((k > 0) & (k < T))
        def _():
            for j in range(NC):
                zrecv(k, j).wait_recv()

                @pl.when(k + 1 < T)
                def _():
                    zsend(k + 1, j).start()

                ysend(k, j).start()
                csend_a(k, j).start()

        @pl.when((k >= 1) & (k < T + 1))
        def _():
            g = k - 1
            s = src_plane(g)
            for j in range(NC):
                xcopy(1, s, 1 - y, c, g, j, e_y).wait_recv()
                csend_b(g, j).start()

            @pl.when(k == 1)
            def _():
                for w in wcopies:
                    w.wait()

            acc = None
            for j in range(NC):
                acc = up_part(s, c, j, acc)
            for j in range(NC):
                xcopy(2, s, y, 1 - c, g, j, e_core).wait_recv()
                xcopy(3, s, 1 - y, 1 - c, g, j, e_core).wait_recv()
                acc = up_part(s, 1 - c, j, acc)
            h0 = act(0, acc[0])
            h1 = act(1, acc[1])
            for j in range(NC):
                def put(lo, hi, v, j=j):
                    ps[g, j, :, lo:hi, :] = v.astype(BF)

                down(h0, h1, 1 - c, j, put)
                psend(g, j).start()
            for j in range(NC):
                def keep(lo, hi, v, j=j):
                    own[j, :, lo:hi, :] = v

                down(h0, h1, c, j, keep)

        @pl.when(k >= 2)
        def _():
            g = k - 2
            for j in range(NC):
                rsend(g, j).wait_recv()
                v = (ks[j] + yr[g, j].astype(F32)).astype(BF)

                @pl.when(g > 0)
                def _():
                    zs[g, j] = v
                    bsend(g, j).start()

                @pl.when(g == 0)
                def _():
                    ret[j, z] = v

        @pl.when((k >= 1) & (k < T + 1))
        def _():
            g = k - 1
            for j in range(NC):
                psend(g, j).wait_recv()
                ys[g, j] = (own[j, 1 - y] + pr[g, j, 1 - y].astype(F32)).astype(BF)
                rsend(g, j).start()
                ks[j] = own[j, y] + pr[g, j, y].astype(F32)

        return carry

    lax.fori_loop(0, T + 2, step, 0)

    orow = pl.ds(pl.multiple_of((1 - c) * TOK, 16), TOK)
    fl = []
    fc = []
    for j in range(NC):
        def got(g, carry, j=j):
            d = dst_plane(g)
            remote(zs.at[g, j], ret.at[j, d], xsend.at[6, g, j], xrecv.at[6, g, j],
                   d * 4 + lax.rem(ep, 4)).wait_recv()
            return carry

        lax.fori_loop(1, T, got, 0)
        back = ret[j].reshape(TR, HC)
        fin[j] = (dot(wt[0], back) + dot(wt[1], back)).astype(BF)

        def cols(i, j=j):
            return pl.ds(pl.multiple_of(i * H + j * HC, 128), HC)

        fc.append(remote(fin.at[j, orow, :], out_ref.at[:, cols(c)], tsend.at[2 + j], trecv.at[2 + j], e_core))
        fc[-1].start()
        fl.append(pltpu.make_async_copy(fin.at[j, mrow, :], out_ref.at[:, cols(c)], lsem.at[1 + j]))
        fl[-1].start()

    def drain(g, carry):
        for j in range(NC):
            @pl.when(g > 0)
            def _():
                zsend(g, j).wait_send()
                bsend(g, j).wait_send()
            ysend(g, j).wait_send()
            csend_a(g, j).wait_send()
            csend_b(g, j).wait_send()
            psend(g, j).wait_send()
            rsend(g, j).wait_send()
        return carry

    lax.fori_loop(0, T, drain, 0)
    tcopy.wait_send()
    mcopy.wait_send()
    for j in range(NC):
        fl[j].wait()
        fc[j].wait_send()
        cc = pl.ds(pl.multiple_of((1 - c) * H + j * HC, 128), HC)
        remote(fin.at[j, orow, :], out_ref.at[:, cc], tsend.at[2 + j], trecv.at[2 + j], e_core).wait_recv()


NC = 2


def solution(mesh):
    devices = mesh.shape["ep"]
    T = devices // 4

    def local(tokens, w_gate_up, w_down, w_copy_gate_up, w_copy_down, routes, gate_weights, counts):
        tok, d = tokens.shape
        hs = w_down.shape[1]
        cap = 5 * tok * routes.shape[1] // (8 * T)
        R = -(-4 * cap // 16) * 16
        lo = 2 * cap // 16 * 16
        hi = -(-2 * cap // 16) * 16
        h = d // 2
        hc = h // NC
        vm = pl.BlockSpec(memory_space=pltpu.VMEM)
        anym = pl.BlockSpec(memory_space=pl.ANY)
        return pl.pallas_call(
            functools.partial(kernel, T, cap, R, lo, hi, NC),
            out_shape=jax.ShapeDtypeStruct((tok, d), BF),
            in_specs=[anym, anym, anym, anym, anym, vm, vm, pl.BlockSpec(memory_space=pltpu.SMEM)],
            out_specs=anym,
            scratch_shapes=[
                pltpu.VMEM((2, d, 2 * hs), BF),
                pltpu.VMEM((2, 2, NC, hs, hc), BF),
                pltpu.VMEM((2 * tok, h), BF),
                pltpu.VMEM((2, 128, 2 * tok), F32),
                pltpu.VMEM((T, NC, R, hc), BF),
                pltpu.VMEM((T, 2, 2, NC, R, hc), BF),
                pltpu.VMEM((3, T * R, 128), BF),
                pltpu.VMEM((T, NC, 2, R, hc), BF),
                pltpu.VMEM((T, NC, 2, R, hc), BF),
                pltpu.VMEM((NC, 2, R, hc), F32),
                pltpu.VMEM((T, NC, R, hc), BF),
                pltpu.VMEM((T, NC, R, hc), BF),
                pltpu.VMEM((NC, R, hc), F32),
                pltpu.VMEM((T, NC, R, hc), BF),
                pltpu.VMEM((NC, T, R, hc), BF),
                pltpu.VMEM((NC, 2 * tok, hc), BF),
                pltpu.VMEM((2, 2 * tok, T * R), BF),
                pltpu.SemaphoreType.DMA((1 + NC,)),
                pltpu.SemaphoreType.DMA((3, 2 * NC)),
                pltpu.SemaphoreType.DMA((7, T, NC)),
                pltpu.SemaphoreType.DMA((7, T, NC)),
                pltpu.SemaphoreType.DMA((2 + NC,)),
                pltpu.SemaphoreType.DMA((2 + NC,)),
            ],
            compiler_params=pltpu.CompilerParams(
                collective_id=0, has_side_effects=True, vmem_limit_bytes=60 * 1024 * 1024
            ),
        )(tokens, w_gate_up, w_down, w_copy_gate_up, w_copy_down, routes.T, gate_weights.T, counts)

    return jax.shard_map(
        local,
        mesh=mesh,
        in_specs=(
            P(("groups", "ep"), None),
            P("ep", None, None),
            P("ep", None, None),
            P("ep", None, None),
            P("ep", None, None),
            P(("groups", "ep"), None),
            P(("groups", "ep"), None),
            P(("groups", "ep")),
        ),
        out_specs=P(("groups", "ep"), None),
        check_vma=False,
    )
```
